32 devices in a mesh: vloop: 4 (over z), pairs: 8 (over y, x, core).
Axes of the slice: x: 2, y: 2, z: 4, core: 2. Of those that a mesh axis runs over, the one named last changes fastest.
Arguments:
- factors: float32 [32, 512, 1280], P('vloop', 'pairs'), may hold values from -0.15625 to 0.15625
- amplitudes: float32 [512, 512, 128], P('vloop', 'pairs'), may hold values from -1 to 1
- occ_energy: float32 [96], replicated, may hold values from -2 to -0.5
- virt_energy: float32 [32], replicated, may hold values from 0.2 to 2.5
- pair_list: int32 [128, 2], P('pairs'), may hold values from 0 to 95
Outputs:
- new_amps: float32 [128, 32, 4, 8], P('pairs', 'vloop')
The draws below stay inside these ranges and needn't reach their ends.
Inputs may be any that keep to these rules, and one draw needn't show every extreme that they name: `pair_list`: each entry names an occupied orbital.
All inputs are finite; a program needn't handle non-finite values.
Results may differ from the reference program's by a relative error of at most 0.00016.
Values sent between devices are 32-bit elements; how exact they have to be, the bound alone decides.
A program may use at most 192 MiB of HBM per device.

```python
import jax
import jax.numpy as jnp
from jax import lax

NO = 96
NV = 512
NAUX = 1280
P_SIZE = 128
ROWS_DEV = 8
STEPS = 4
ROWS = 32


def plant(array, rng, low, high):
    extent = array.shape
    index_at = [jax.random.randint(jax.random.fold_in(rng, axis), (), 0, extent[axis]) for axis in range(len(extent))]
    array = array.at[tuple(index_at)].set(low)
    longest = extent.index(max(extent))
    index_at[longest] = (index_at[longest] + 1) % extent[longest]
    return array.at[tuple(index_at)].set(high)


def block_levels(stream_key, shape, shards, least, high):
    gain, own = 1.0, jax.random.fold_in(stream_key, 6)
    for axis_at, blocks in shards:
        draws = jnp.exp(jax.random.uniform(jax.random.fold_in(own, axis_at), (blocks,), jnp.float32, least / len(shards), high / len(shards)))
        gain = gain * jnp.repeat(draws, shape[axis_at] // blocks).reshape([-1 if axis == axis_at else 1 for axis in range(len(shape))])
    return gain


def centred(key, dims, deviation, most, shards=(), held_as=jnp.bfloat16):
    gain = block_levels(key, dims, shards, -0.22, 0.18) if shards else 1.0
    result = jax.random.normal(key, dims, jnp.float32) * deviation * gain
    return jnp.minimum(jnp.maximum(result, -most), most).astype(held_as)


def setup_inputs(seed: int = 0) -> dict:
    key_list = jax.random.split(jax.random.key(seed), 6)
    return {
        "factors": centred(key_list[0], (ROWS, NV, NAUX), NAUX ** -0.5, 0.15625, ((0, 4), (1, 8)), jnp.float32),
        "amplitudes": centred(key_list[1], (NV, NV, P_SIZE), 0.15, 1.0, ((0, 4), (1, 8)), jnp.float32),
        "occ_energy": jnp.clip(jax.random.uniform(key_list[2], (NO,), jnp.float32, -2.0, -0.5), -2.0, -0.5),
        "virt_energy": jnp.clip(jax.random.uniform(key_list[3], (ROWS,), jnp.float32, 0.2, 2.5), 0.2, 2.5),
        "pair_list": plant(jax.random.randint(key_list[4], (P_SIZE, 2), 0, NO), jax.random.fold_in(key_list[4], 1), 0, NO - 1).astype(jnp.int32),
    }


def reference(factors, amplitudes, occ_energy, virt_energy, pair_list):
    blocks = ROWS // ROWS_DEV
    factor_blocks = factors.reshape(blocks, ROWS_DEV, NV, NAUX)
    occ_pair = occ_energy[pair_list[:, 0]] + occ_energy[pair_list[:, 1]]
    virt_blocks = virt_energy.reshape(blocks, ROWS_DEV)
    step_terms = []
    partner_energy = []
    for step_index in range(STEPS):
        partner = jnp.roll(factor_blocks, step_index, axis=0)

        def per_block(block_index):
            row_side = lax.dynamic_index_in_dim(factor_blocks, block_index, 0, keepdims=False)
            col_side = lax.dynamic_index_in_dim(partner, block_index, 0, keepdims=False)
            integrals = lax.dot_general(row_side.reshape(ROWS_DEV * NV, NAUX), col_side.reshape(ROWS_DEV * NV, NAUX), (((1,), (1,)), ((), ())), precision=lax.Precision.HIGHEST, preferred_element_type=jnp.float32)
            integrals = integrals.reshape(ROWS_DEV, NV, ROWS_DEV, NV)
            return jnp.einsum("acbd,cdp->pab", integrals, amplitudes, precision=lax.Precision.HIGHEST)

        block_terms = lax.map(per_block, jnp.arange(blocks, dtype=jnp.int32))
        step_terms.append(block_terms)
        partner_energy.append(jnp.roll(virt_blocks, step_index, axis=0))
    stacked = jnp.stack(step_terms, axis=0)
    ladder = jnp.transpose(stacked, (2, 1, 3, 0, 4)).reshape(P_SIZE, ROWS, STEPS, ROWS_DEV)
    energy_b = jnp.stack(partner_energy, axis=1)
    energy_b = jnp.broadcast_to(energy_b[:, None, :, :], (blocks, ROWS_DEV, STEPS, ROWS_DEV)).reshape(ROWS, STEPS, ROWS_DEV)
    denominator = virt_energy[None, :, None, None] + energy_b[None] - occ_pair[:, None, None, None]
    return ladder / denominator
```

```python
import functools

import jax
import jax.numpy as jnp
from jax import lax
from jax.experimental import pallas as pl
from jax.experimental.pallas import tpu as pltpu
from jax.sharding import PartitionSpec as P

STEPS = 4
LANES = 128
WIDE = 256
NT = (((1,), (1,)), ((), ()))
NN = (((1,), (0,)), ((), ()))


def split(value):
    high = value.astype(jnp.bfloat16)
    return high, (value - high.astype(jnp.float32)).astype(jnp.bfloat16)


def product(left, right, dims):
    dot = functools.partial(
        lax.dot_general, dimension_numbers=dims, preferred_element_type=jnp.float32
    )
    return dot(left[0], right[0]) + (dot(left[0], right[1]) + dot(left[1], right[0]))


def ladder_kernel(count, row_ref, amp_ref, *refs):
    cols, (out_ref, high_ref, low_ref, held_ref) = refs[:count], refs[count:]
    rows, tile, aux = row_ref.shape
    width = cols[0].shape[0]
    depth = amp_ref.shape[1]
    group = LANES // depth
    fold = WIDE // LANES

    @pl.when(pl.program_id(0) == 0)
    def _():
        out_ref[...] = jnp.zeros_like(out_ref)
        for i in range(count):
            high, low = split(cols[i][...])
            high_ref[pl.ds(i * width, width), :] = high
            low_ref[pl.ds(i * width, width), :] = low

    left = split(row_ref[...].reshape(rows * tile, aux))
    for i in range(count):
        at = pl.ds(i * width, width)
        part = product(left, (high_ref[at, :], low_ref[at, :]), NT)
        for b in range(width // LANES):
            held_ref[i * (width // LANES) + b] = part[:, b * LANES : (b + 1) * LANES]

    total = out_ref[...]
    for c in range(0, tile, fold):
        weights = []
        for k in range(fold):
            amp = amp_ref[c + k]
            blank = jnp.zeros_like(amp)
            for g in range(group):
                weights.append(
                    jnp.concatenate([amp if h == g else blank for h in range(group)], axis=1)
                )
        right = split(jnp.concatenate(weights, axis=0))
        pieces = []
        for b in range(count * width // LANES):
            pieces.append(
                jnp.concatenate(
                    [
                        held_ref[b, pl.ds(c + k, rows, stride=tile), :]
                        for k in range(fold)
                    ],
                    axis=1,
                )
            )
        total = total + product(split(jnp.concatenate(pieces, axis=0)), right, NN)
    out_ref[...] = total


def ladder_part(row_side, amplitudes, cols):
    rows, all_c, aux = row_side.shape
    _, depth, pair_count = amplitudes.shape
    count = len(cols)
    width = cols[0].shape[0] * cols[0].shape[1]
    group = LANES // depth
    tile = max(8, 512 // rows)
    height = count * width // LANES * rows
    out = pl.pallas_call(
        functools.partial(ladder_kernel, count),
        grid=(all_c // tile,),
        out_shape=jax.ShapeDtypeStruct((height, group * pair_count), jnp.float32),
        in_specs=[
            pl.BlockSpec((rows, tile, aux), lambda i: (0, i, 0)),
            pl.BlockSpec((tile, depth, pair_count), lambda i: (i, 0, 0)),
        ]
        + [
            pl.BlockSpec((width, aux), lambda i: (0, 0), pipeline_mode=pl.Buffered(1))
        ] * count,
        out_specs=pl.BlockSpec((height, group * pair_count), lambda i: (0, 0)),
        scratch_shapes=[
            pltpu.VMEM((count * width, aux), jnp.bfloat16),
            pltpu.VMEM((count * width, aux), jnp.bfloat16),
            pltpu.VMEM((count * width // LANES, rows * tile, LANES), jnp.float32),
        ],
        compiler_params=pltpu.CompilerParams(vmem_limit_bytes=56 * 2**20),
        cost_estimate=pl.CostEstimate(
            flops=6 * rows * all_c * count * width * (aux + group * pair_count),
            bytes_accessed=4 * (rows * all_c * aux + count * width * aux),
            transcendentals=0,
        ),
    )(row_side, amplitudes, *[col.reshape(width, aux) for col in cols])
    out = out.reshape(count * width // LANES, rows, group, pair_count)
    return out.transpose(0, 2, 1, 3).reshape(count, -1, rows, pair_count)


def local(factors, amplitudes, occ_energy, virt_energy, pair_list):
    loop_size = lax.axis_size("vloop")
    pair_size = lax.axis_size("pairs")
    loop_index = lax.axis_index("vloop")
    rows_dev, slice_cols, aux_count = factors.shape
    pair_count = amplitudes.shape[2]
    block_cols = amplitudes.shape[0]
    per_block = pair_size // loop_size
    rows_each = max(1, rows_dev // pair_size)
    cols_each = rows_dev * slice_cols // (pair_size * rows_each)
    chunk = rows_each * cols_each

    spread = lax.all_to_all(factors.reshape(pair_size, chunk, aux_count), "pairs", 0, 0)
    spread = lax.all_to_all(
        spread.reshape(loop_size, per_block, chunk, aux_count), "vloop", 0, 0
    )
    row_side = lax.all_gather(
        spread.reshape(loop_size, 1, per_block * chunk, aux_count), "pairs", axis=1, tiled=True
    )
    row_side = row_side.reshape(
        loop_size,
        rows_dev // rows_each,
        slice_cols // cols_each,
        per_block,
        rows_each,
        cols_each,
        aux_count,
    )
    row_side = row_side.transpose(0, 1, 4, 3, 2, 5, 6)
    row_side = row_side.reshape(loop_size * rows_dev, block_cols, aux_count)

    def shifted(by):
        if by == 0:
            return factors
        return lax.ppermute(factors, "vloop", [(i, (i + by) % loop_size) for i in range(loop_size)])

    order = [0, 1, loop_size - 1] + list(range(2, loop_size - 1))
    half = loop_size // 2
    found = {}
    for start in (0, half):
        shifts = order[start : start + half]
        part = ladder_part(row_side, amplitudes, [shifted(by) for by in shifts])
        for i, by in enumerate(shifts):
            found[by] = part[i]
    stacked = jnp.stack([found[by] for by in range(loop_size)])
    blocks = [
        lax.dynamic_index_in_dim(stacked, jnp.mod(loop_index - w + loop_size, loop_size), 0, False)
        for w in range(loop_size)
    ]
    rows = []
    for z in range(loop_size):
        mine = jnp.stack([blocks[(z - s) % loop_size] for s in range(STEPS)])
        mine = mine[:, :, z * rows_dev : (z + 1) * rows_dev]
        rows.append(mine.transpose(3, 2, 0, 1))
    ladder = jnp.concatenate(rows, axis=1)
    summed = lax.psum_scatter(ladder, "pairs", scatter_dimension=0, tiled=True)
    summed = lax.psum_scatter(summed, "vloop", scatter_dimension=1, tiled=True)

    one_hot = (
        pair_list[:, :, None] == jnp.arange(occ_energy.shape[0], dtype=jnp.int32)[None, None, :]
    ).astype(jnp.float32)
    occ_pair = jnp.sum(one_hot * occ_energy[None, None, :], axis=(1, 2))
    energy_a = lax.dynamic_slice_in_dim(virt_energy, loop_index * rows_dev, rows_dev)
    partner_list = []
    for step_index in range(STEPS):
        owner_block = jnp.mod(loop_index - step_index + loop_size, loop_size)
        partner_list.append(lax.dynamic_slice_in_dim(virt_energy, owner_block * rows_dev, rows_dev))
    energy_b = jnp.stack(partner_list, axis=0)
    denominator = (
        energy_a[None, :, None, None] + energy_b[None, None, :, :] - occ_pair[:, None, None, None]
    )
    return summed / denominator


def solution(mesh):
    placed = (P("vloop", "pairs", None), P("vloop", "pairs", None), P(), P(), P("pairs", None))
    return jax.shard_map(
        local,
        mesh=mesh,
        in_specs=placed,
        out_specs=P("pairs", "vloop", None, None),
        check_vma=False,
    )
```

```python
import functools

import jax
import jax.numpy as jnp
from jax import lax
from jax.experimental import pallas as pl
from jax.experimental.pallas import tpu as pltpu
from jax.sharding import PartitionSpec as P

STEPS = 4
LANES = 128
WIDE = 256
NT = (((1,), (1,)), ((), ()))
NN = (((1,), (0,)), ((), ()))


def split(value):
    high = value.astype(jnp.bfloat16)
    return high, (value - high.astype(jnp.float32)).astype(jnp.bfloat16)


def product(left, right, dims):
    dot = functools.partial(
        lax.dot_general, dimension_numbers=dims, preferred_element_type=jnp.float32
    )
    return dot(left[0], right[0]) + (dot(left[0], right[1]) + dot(left[1], right[0]))


def ladder_kernel(count, row_ref, amp_ref, *refs):
    cols, (out_ref, high_ref, low_ref, held_ref) = refs[:count], refs[count:]
    rows, tile, aux = row_ref.shape
    width = cols[0].shape[0]
    depth = amp_ref.shape[1]
    group = LANES // depth
    fold = WIDE // LANES

    @pl.when(pl.program_id(0) == 0)
    def _():
        out_ref[...] = jnp.zeros_like(out_ref)
        for i in range(count):
            high, low = split(cols[i][...])
            high_ref[pl.ds(i * width, width), :] = high
            low_ref[pl.ds(i * width, width), :] = low

    left = split(row_ref[...].reshape(rows * tile, aux))
    for i in range(count):
        at = pl.ds(i * width, width)
        part = product(left, (high_ref[at, :], low_ref[at, :]), NT)
        for b in range(width // LANES):
            held_ref[i * (width // LANES) + b] = part[:, b * LANES : (b + 1) * LANES]

    total = out_ref[...]
    for c in range(0, tile, fold):
        weights = []
        for k in range(fold):
            amp = amp_ref[c + k]
            blank = jnp.zeros_like(amp)
            for g in range(group):
                weights.append(
                    jnp.concatenate([amp if h == g else blank for h in range(group)], axis=1)
                )
        right = split(jnp.concatenate(weights, axis=0))
        pieces = []
        for b in range(count * width // LANES):
            pieces.append(
                jnp.concatenate(
                    [
                        held_ref[b, pl.ds(c + k, rows, stride=tile), :]
                        for k in range(fold)
                    ],
                    axis=1,
                )
            )
        total = total + product(split(jnp.concatenate(pieces, axis=0)), right, NN)
    out_ref[...] = total


def ladder_part(row_side, amplitudes, cols):
    rows, all_c, aux = row_side.shape
    _, depth, pair_count = amplitudes.shape
    count = len(cols)
    width = cols[0].shape[0] * cols[0].shape[1]
    group = LANES // depth
    tile = max(8, 512 // rows)
    height = count * width // LANES * rows
    out = pl.pallas_call(
        functools.partial(ladder_kernel, count),
        grid=(all_c // tile,),
        out_shape=jax.ShapeDtypeStruct((height, group * pair_count), jnp.float32),
        in_specs=[
            pl.BlockSpec((rows, tile, aux), lambda i: (0, i, 0)),
            pl.BlockSpec((tile, depth, pair_count), lambda i: (i, 0, 0)),
        ]
        + [
            pl.BlockSpec((width, aux), lambda i: (0, 0), pipeline_mode=pl.Buffered(1))
        ] * count,
        out_specs=pl.BlockSpec((height, group * pair_count), lambda i: (0, 0)),
        scratch_shapes=[
            pltpu.VMEM((count * width, aux), jnp.bfloat16),
            pltpu.VMEM((count * width, aux), jnp.bfloat16),
            pltpu.VMEM((count * width // LANES, rows * tile, LANES), jnp.float32),
        ],
        compiler_params=pltpu.CompilerParams(vmem_limit_bytes=56 * 2**20),
        cost_estimate=pl.CostEstimate(
            flops=6 * rows * all_c * count * width * (aux + group * pair_count),
            bytes_accessed=4 * (rows * all_c * aux + count * width * aux),
            transcendentals=0,
        ),
    )(row_side, amplitudes, *[col.reshape(width, aux) for col in cols])
    out = out.reshape(count * width // LANES, rows, group, pair_count)
    return out.transpose(0, 2, 1, 3).reshape(count, -1, rows, pair_count)


def local(factors, amplitudes, occ_energy, virt_energy, pair_list):
    loop_size = lax.axis_size("vloop")
    pair_size = lax.axis_size("pairs")
    loop_index = lax.axis_index("vloop")
    rows_dev, slice_cols, aux_count = factors.shape
    pair_count = amplitudes.shape[2]
    block_cols = amplitudes.shape[0]
    per_block = pair_size // loop_size
    rows_each = max(1, rows_dev // pair_size)
    cols_each = rows_dev * slice_cols // (pair_size * rows_each)
    chunk = rows_each * cols_each

    spread = lax.all_to_all(factors.reshape(pair_size, chunk, aux_count), "pairs", 0, 0)
    spread = lax.all_to_all(
        spread.reshape(loop_size, per_block, chunk, aux_count), "vloop", 0, 0
    )
    row_side = lax.all_gather(
        spread.reshape(loop_size, 1, per_block * chunk, aux_count), "pairs", axis=1, tiled=True
    )
    row_side = row_side.reshape(
        loop_size,
        rows_dev // rows_each,
        slice_cols // cols_each,
        per_block,
        rows_each,
        cols_each,
        aux_count,
    )
    row_side = row_side.transpose(0, 1, 4, 3, 2, 5, 6)
    row_side = row_side.reshape(loop_size * rows_dev, block_cols, aux_count)

    def shifted(block, by):
        return lax.ppermute(block, "vloop", [(i, (i + by) % loop_size) for i in range(loop_size)])

    order = [0, 1, loop_size - 1] + list(range(2, loop_size - 1))
    blocks_of = {0: factors, 1: shifted(factors, 1), loop_size - 1: shifted(factors, -1)}
    for by in range(2, loop_size - 1):
        blocks_of[by] = shifted(blocks_of[by - 1], 1)
    half = loop_size // 2
    found = {}
    for start in (0, half):
        shifts = order[start : start + half]
        part = ladder_part(row_side, amplitudes, [blocks_of[by] for by in shifts])
        part, amplitudes = lax.optimization_barrier((part, amplitudes))
        for i, by in enumerate(shifts):
            found[by] = part[i]
    stacked = jnp.stack([found[by] for by in range(loop_size)])
    blocks = [
        lax.dynamic_index_in_dim(stacked, jnp.mod(loop_index - w + loop_size, loop_size), 0, False)
        for w in range(loop_size)
    ]
    rows = []
    for z in range(loop_size):
        mine = jnp.stack([blocks[(z - s) % loop_size] for s in range(STEPS)])
        mine = mine[:, :, z * rows_dev : (z + 1) * rows_dev]
        rows.append(mine)
    ladder = lax.all_to_all(jnp.stack(rows), "vloop", 0, 0)
    summed = jnp.sum(ladder, axis=0).reshape(-1, rows_dev, pair_count)
    summed = summed.transpose(2, 1, 0).reshape(pair_size, pair_count // pair_size, -1)
    summed = jnp.sum(lax.all_to_all(summed, "pairs", 0, 0), axis=0)
    summed = summed.reshape(-1, rows_dev, STEPS, rows_dev)

    one_hot = (
        pair_list[:, :, None] == jnp.arange(occ_energy.shape[0], dtype=jnp.int32)[None, None, :]
    ).astype(jnp.float32)
    occ_pair = jnp.sum(one_hot * occ_energy[None, None, :], axis=(1, 2))
    energy_a = lax.dynamic_slice_in_dim(virt_energy, loop_index * rows_dev, rows_dev)
    partner_list = []
    for step_index in range(STEPS):
        owner_block = jnp.mod(loop_index - step_index + loop_size, loop_size)
        partner_list.append(lax.dynamic_slice_in_dim(virt_energy, owner_block * rows_dev, rows_dev))
    energy_b = jnp.stack(partner_list, axis=0)
    denominator = (
        energy_a[None, :, None, None] + energy_b[None, None, :, :] - occ_pair[:, None, None, None]
    )
    return summed / denominator


def solution(mesh):
    placed = (P("vloop", "pairs", None), P("vloop", "pairs", None), P(), P(), P("pairs", None))
    return jax.shard_map(
        local,
        mesh=mesh,
        in_specs=placed,
        out_specs=P("pairs", "vloop", None, None),
        check_vma=False,
    )
```
